512 devices in a mesh: grp: 8 (over z), dev: 64 (over x, y, core).
Axes of the slice: x: 4, y: 8, z: 8, core: 2. Of those that a mesh axis runs over, the one named last changes fastest.
Arguments:
- points: float32 [3, 1048576], P(None, ('grp', 'dev')), may hold values from 0 to 16, as said below
- probes: float32 [1048576, 256], P(('grp', 'dev')), may hold values from -6 to 6
- samples: float32 [1048576, 256], P(('grp', 'dev')), may hold values from -60 to 60
- near_mask: int32 [2048, 4], P(('grp', 'dev')), may hold values 0 or 1
Outputs:
- leaf_basis: bfloat16 [1048576, 128], P(('grp', 'dev'))
- coupling: bfloat16 [262144, 128], P(('grp', 'dev'))
- parent_basis: float32 [262144, 128], P(('grp', 'dev'))
The draws below stay inside these ranges and needn't reach their ends.
Inputs may be any that keep to these rules, and one draw needn't show every extreme that they name: `points`: coordinates lie in the unit cells of a grid of cells, leaf t in the cell given by the bits of t taken in turn for the three coordinates.
All inputs are finite; a program needn't handle non-finite values. No bound on the sum of `near_mask` on one device may be relied on, other than what follows from the above.
Results may differ from the reference program's by a relative error of at most 0.0018.
Values sent between devices are 32-bit elements; how exact they have to be, the bound alone decides.
No kernel may reach another device: no remote copies, remote signals or barrier semaphores. Data moves between devices by JAX's collectives and lax.ppermute only.
A program may use at most 64 MiB of HBM per device.

```python
import math
import jax
import jax.numpy as jnp
from jax import lax

LEAF = 512
PROBES = 256
KL = 128
KP = 128
LEAVES = 2048
POINTS = 1048576


def draw_points(key, part):
    key = jax.random.fold_in(key, 11)
    leaf_index = jnp.arange(POINTS, dtype=jnp.int32) // LEAF
    bit_count = max(LEAVES.bit_length() - 1, 0)
    coordinates = []
    for dimension in range(3):
        cell_index = jnp.zeros((POINTS,), jnp.int32)
        for bit_number in range(dimension, bit_count, 3):
            cell_index = cell_index + (leaf_index >> bit_number & 1) * 2 ** (bit_number // 3)
        coordinates.append(cell_index.astype(jnp.float32))
    cells = jnp.stack(coordinates)
    inside = jax.random.uniform(key, (3, POINTS), dtype=jnp.float32)
    return cells + inside


def draw_samples(key, part):
    key = jax.random.fold_in(key, 23)
    row_key, column_key, value_key = jax.random.split(key, 3)
    row_scale = jnp.exp(jax.random.uniform(row_key, (POINTS, 1), minval=math.log(0.5), maxval=math.log(5.0)))
    column_scale = jnp.exp(jax.random.uniform(column_key, (1, PROBES), minval=math.log(0.5), maxval=math.log(2.0)))
    values = jax.random.truncated_normal(value_key, -4.0, 4.0, (POINTS, PROBES))
    return (1.5 * row_scale * column_scale * values).astype(jnp.float32)


def set_ends(entries, rng, smallest, top_value):
    longest = entries.shape.index(max(entries.shape))
    spots = []
    for shift in (0, 1):
        where = [jax.random.randint(jax.random.fold_in(rng, axis), (), 0, length) for axis, length in enumerate(entries.shape)]
        where[longest] = (where[longest] + shift) % entries.shape[longest]
        spots.append(tuple(where))
    return entries.at[spots[0]].set(smallest).at[spots[1]].set(top_value)


def block_levels(stream_key, dims, cuts, least, high):
    def one(axis_at, blocks):
        draws = jax.random.uniform(jax.random.fold_in(jax.random.fold_in(stream_key, 6), axis_at), (blocks,), jnp.float32, least / len(cuts), high / len(cuts))
        return jnp.repeat(jnp.exp(draws), dims[axis_at] // blocks).reshape((-1,) + (1,) * (len(dims) - axis_at - 1))

    level = one(*cuts[0])
    for cut in cuts[1:]:
        level = level * one(*cut)
    return level


def scatter_about(key, shape, width, limit, cuts=(), kind=jnp.bfloat16):
    array = width * jax.random.normal(key, shape, jnp.float32)
    if cuts:
        array = array * block_levels(key, shape, cuts, -0.22, 0.18)
    return jnp.clip(array, -limit, limit).astype(kind)


def setup_inputs(seed: int = 0) -> dict:
    seeds = jax.random.split(jax.random.key(seed), 5)
    points = draw_points(jax.random.fold_in(seeds[4], 71), 0)
    probes = scatter_about(seeds[1], (POINTS, PROBES), 1.0, 6.0, ((0, 512),), jnp.float32)
    samples = draw_samples(jax.random.fold_in(seeds[4], 71), 0)
    near_mask = set_ends((jax.random.randint(seeds[3], (LEAVES, 4), 0, 4) < 3).astype(jnp.int32), jax.random.fold_in(seeds[3], 1), 0, 1)
    return {"points": points, "probes": probes, "samples": samples, "near_mask": near_mask}


highest = lax.Precision.HIGHEST
amplitude = 0.25
length_scale = 1.0
shift_ratio = 0.01
epsilon = 1e-05
neighbour_offsets = (-2, -1, 1, 2)

def matern(targets, sources):
    squared = jnp.zeros((targets.shape[1], sources.shape[1]), targets.dtype)
    for dimension in range(3):
        spread = targets[dimension][:, None] - sources[dimension][None, :]
        squared = squared + spread * spread
    scaled = math.sqrt(3.0) / length_scale * jnp.sqrt(squared)
    return amplitude * (1.0 + scaled) * jnp.exp(-scaled)

def shifted_cholesky(gram_matrix):
    order = gram_matrix.shape[0]
    diag_level = jnp.trace(gram_matrix) / order
    identity = jnp.eye(order, dtype=gram_matrix.dtype)
    return jnp.linalg.cholesky(gram_matrix + (shift_ratio * diag_level + epsilon) * identity)

def right_solve(factor, values):
    return lax.linalg.triangular_solve(factor, values, left_side=False, lower=True, transpose_a=True)

def orthonormal_columns(columns_block):
    gram_matrix = jnp.dot(columns_block.T, columns_block, precision=highest) / columns_block.shape[0]
    return right_solve(shifted_cholesky(gram_matrix), columns_block)

def probe_factor(reduced_probes):
    gram_matrix = jnp.dot(reduced_probes, reduced_probes.T, precision=highest) / reduced_probes.shape[1]
    return shifted_cholesky(gram_matrix)

def couple(reduced_samples, sibling_probes, sibling_factor):
    cross = jnp.dot(reduced_samples, sibling_probes.T, precision=highest) / sibling_probes.shape[1]
    halfway = right_solve(sibling_factor, cross)
    coupling = lax.linalg.triangular_solve(sibling_factor, halfway, left_side=False, lower=True, transpose_a=False)
    remainder = reduced_samples - jnp.dot(coupling, sibling_probes, precision=highest)
    return (coupling, remainder)

def local_gram(parent_rows):
    return jnp.dot(parent_rows.T, parent_rows, precision=highest)

def reference(points, probes, samples, near_mask):
    leaf_points = points.reshape(3, LEAVES, LEAF).transpose(1, 0, 2)
    leaf_probes = probes.reshape(LEAVES, LEAF, PROBES)
    leaf_samples = samples.reshape(LEAVES, LEAF, PROBES)
    padded_points = jnp.pad(leaf_points, ((2, 2), (0, 0), (0, 0)))
    padded_probes = jnp.pad(leaf_probes, ((2, 2), (0, 0), (0, 0)))

    def one_leaf(position):
        own_points = leaf_points[position]
        own_probes = leaf_probes[position]
        remaining = leaf_samples[position] - jnp.dot(matern(own_points, own_points), own_probes, precision=highest)
        for slot_index, offset in enumerate(neighbour_offsets):
            other_points = padded_points[position + 2 + offset]
            other_probes = padded_probes[position + 2 + offset]
            weight = near_mask[position, slot_index].astype(samples.dtype)
            remaining = remaining - weight * jnp.dot(matern(own_points, other_points), other_probes, precision=highest)
        basis = orthonormal_columns(remaining[:, :KL])
        reduced_samples = jnp.dot(basis.T, remaining, precision=highest) / LEAF
        reduced_probes = jnp.dot(basis.T, own_probes, precision=highest) / math.sqrt(LEAF)
        return (basis, reduced_samples, reduced_probes)
    basis, reduced_samples, reduced_probes = lax.map(one_leaf, jnp.arange(LEAVES, dtype=jnp.int32))
    sibling = jnp.arange(LEAVES, dtype=jnp.int32) ^ 1
    sibling_probes = reduced_probes[sibling]
    factors = jax.vmap(probe_factor)(sibling_probes)
    coupling, remainder = jax.vmap(couple)(reduced_samples, sibling_probes, factors)
    parent_rows = remainder[:, :, :KP]
    grams = jax.vmap(local_gram)(parent_rows)
    node_gram = grams.sum(axis=0) / (LEAVES * KL)
    node_factor = shifted_cholesky(node_gram)
    parent_basis = jax.vmap(right_solve, in_axes=(None, 0))(node_factor, parent_rows)
    return (basis.reshape(POINTS, KL).astype(jnp.bfloat16), coupling.reshape(LEAVES * KL, KL).astype(jnp.bfloat16), parent_basis.reshape(LEAVES * KL, KP))
```

```python
import math

import jax
import jax.numpy as jnp
from jax import lax
from jax.experimental import pallas as pl
from jax.experimental.pallas import tpu as pltpu
from jax.sharding import Mesh, PartitionSpec as P

LEAF = 512
COLS = 256
KL = 128
COUNT = 4
LEAVES = 2048
FEATURES = 32
PANEL = 16
ROWS = 128

AMPLITUDE = 0.25
SHIFT_RATIO = 0.01
EPSILON = 1e-05
LOG2E = math.log2(math.e)
SCALE = math.sqrt(3.0) * LOG2E
WEIGHT = AMPLITUDE / LOG2E

highest = lax.Precision.HIGHEST
f32 = jnp.float32
bf16 = jnp.bfloat16
AXES = ("z", "x", "y", "c")
VMEM_LIMIT = 48 * 1024 * 1024


def split2(values):
    high = values.astype(bf16)
    low = (values - high.astype(f32)).astype(bf16)
    return high, low


def split3(values):
    high = values.astype(bf16)
    rest = values - high.astype(f32)
    middle = rest.astype(bf16)
    low = (rest - middle.astype(f32)).astype(bf16)
    return high, middle, low


def dot(left, right, contract, precision=highest):
    return lax.dot_general(
        left, right, ((contract[:1], contract[1:]), ((), ())),
        precision=precision, preferred_element_type=f32,
    )


def fast(left, right, contract):
    return dot(left, right, contract, None)


def features(points, target):
    rows = [points[d : d + 1, :] for d in range(3)]
    norm = [piece.astype(f32) for piece in split3(rows[0] * rows[0] + rows[1] * rows[1] + rows[2] * rows[2])]
    ones = jnp.ones_like(rows[0])
    out = []
    for row in rows:
        pieces = [piece.astype(f32) for piece in split3(row)]
        if target:
            out += [pieces[i] for i in (0, 0, 1, 1, 0, 2)]
        else:
            out += [-2.0 * pieces[i] for i in (0, 1, 0, 1, 2, 0)]
    out += norm + [ones] * 3 if target else [ones] * 3 + norm
    out += [jnp.zeros_like(ones)] * (FEATURES - len(out))
    return jnp.concatenate(out, axis=0)


def block_product(targets_ref, sources_ref, high_ref, low_ref, target, source, step):
    columns = pl.ds(pl.multiple_of(source * LEAF, LEAF), LEAF)
    kernel_sources = sources_ref[:, columns]
    high_probes = high_ref[columns, :]
    low_probes = low_ref[columns, :]
    for part in range(LEAF // ROWS):
        rows = pl.ds(pl.multiple_of(target * LEAF + part * ROWS, ROWS), ROWS)
        squared = fast(targets_ref[rows, :], kernel_sources, (1, 0))
        squared = jnp.maximum(squared, 1e-24)
        scaled = squared * lax.rsqrt(squared)
        high, low = split2((scaled + LOG2E) * jnp.exp2(-scaled))
        product = fast(high, high_probes, (1, 0)) + fast(low, high_probes, (1, 0)) + fast(high, low_probes, (1, 0))
        step(rows, product)


def local_kernel(mask_ref, points_ref, probes_ref, samples_ref, out_ref, targets_ref, sources_ref, high_ref, low_ref):
    centred = (points_ref[...] - points_ref[:, 0:1]) * SCALE
    targets_ref[...] = features(centred, True).T.astype(bf16)
    sources_ref[...] = features(centred, False).astype(bf16)
    high, low = split2(probes_ref[...])
    high_ref[...] = high
    low_ref[...] = low
    out_ref[...] = samples_ref[...]

    def target_loop(target, _):
        def source_loop(source, _):
            offset = source - target
            slot = jnp.clip(jnp.where(offset < 0, offset + 2, offset + 1), 0, 3)
            weight = jnp.where(offset == 0, 1, mask_ref[target, slot]).astype(f32) * WEIGHT

            def step(rows, product):
                out_ref[rows, :] -= weight * product

            block_product(targets_ref, sources_ref, high_ref, low_ref, target, source, step)
            return 0

        return lax.fori_loop(jnp.maximum(target - 2, 0), jnp.minimum(target + 3, COUNT), source_loop, 0)

    lax.fori_loop(0, COUNT, target_loop, 0)


def shifted_gram(gram):
    row = lax.broadcasted_iota(jnp.int32, (KL, KL), 0)
    column = lax.broadcasted_iota(jnp.int32, (KL, KL), 1)
    diagonal = row == column
    trace = jnp.sum(jnp.where(diagonal, gram, 0.0))
    return gram + jnp.where(diagonal, SHIFT_RATIO * trace / KL + EPSILON, 0.0)


def inverse_factors(work_ref, panel_ref, number):
    lane = lax.broadcasted_iota(jnp.int32, (number, KL), 1)
    wide_lane = lax.broadcasted_iota(jnp.int32, (KL, KL), 1)
    for first in range(0, KL, PANEL):
        rows = [work_ref[pl.ds(first + j, number, stride=KL), :] for j in range(PANEL)]
        entry = {
            (j, i): jnp.broadcast_to(rows[j][:, first + i : first + i + 1], (number, KL))
            for j in range(PANEL)
            for i in range(j, PANEL)
        }
        inside = (lane >= first) & (lane < first + PANEL)
        rows = [jnp.where(inside, jnp.where(lane == first + j, 1.0, 0.0), rows[j]) for j in range(PANEL)]
        for k in range(PANEL):
            scale = lax.rsqrt(entry[k, k])
            rows[k] = rows[k] * scale
            factor = {j: entry[k, j] * scale for j in range(k + 1, PANEL)}
            for j in range(k + 1, PANEL):
                for i in range(j, PANEL):
                    entry[j, i] = entry[j, i] - factor[j] * factor[i]
                rows[j] = rows[j] - factor[j] * rows[k]
            panel_ref[pl.ds(k, number, stride=PANEL), :] = rows[k]
        after = first + PANEL
        for matrix in range(number):
            panel = panel_ref[matrix * PANEL : (matrix + 1) * PANEL, :]
            base = matrix * KL
            work_ref[base + first : base + after, :] = jnp.where(
                wide_lane[:PANEL] < after, panel, 0.0
            )
            if after < KL:
                high, middle, low = split3(panel)
                left = jnp.concatenate([high, high, middle, middle, high, low], axis=0)
                right = jnp.concatenate([high, middle, high, middle, low, high], axis=0)
                update = fast(left, right, (0, 0))
                done = (wide_lane >= first) & (wide_lane < after)
                old = jnp.where(done[after:], 0.0, work_ref[base + after : base + KL, :])
                work_ref[base + after : base + KL, :] = old - update[after:, :]


def halo_kernel(
    mask_ref, points_ref, before_points_ref, after_points_ref, partial_ref, probes_ref, before_ref, after_ref,
    basis_ref, coupling_ref, parent_ref, gram_ref,
    targets_ref, sources_ref, high_ref, low_ref, remaining_ref, work_ref, panel_ref,
):
    centre = points_ref[:, 0:1]
    targets_ref[...] = features((points_ref[...] - centre) * SCALE, True).T.astype(bf16)
    for half, (halo_points, halo_probes) in enumerate(((before_points_ref, before_ref), (after_points_ref, after_ref))):
        columns = slice(half * 2 * LEAF, (half + 1) * 2 * LEAF)
        sources_ref[:, columns] = features((halo_points[...] - centre) * SCALE, False).astype(bf16)
        high, low = split2(halo_probes[...])
        high_ref[columns, :] = high
        low_ref[columns, :] = low
    remaining_ref[...] = partial_ref[...]

    def pair_loop(pair, _):
        source = (pair + 1) // 2
        target = pair - jnp.where(pair >= 1, 1, 0) - jnp.where(pair >= 5, 1, 0)
        offset = jnp.where(source < 2, source - 2, source + 2) - target
        slot = jnp.where(offset < 0, offset + 2, offset + 1)
        weight = mask_ref[target, slot].astype(f32) * WEIGHT

        def step(rows, product):
            remaining_ref[rows, :] -= weight * product

        block_product(targets_ref, sources_ref, high_ref, low_ref, target, source, step)
        return 0

    lax.fori_loop(0, 6, pair_loop, 0)

    samples_products, probes_products = [], []
    for leaf in range(COUNT):
        rows = slice(leaf * LEAF, (leaf + 1) * LEAF)
        block = remaining_ref[rows, :KL]
        samples_products.append(dot(block, remaining_ref[rows, :], (0, 0)))
        probes_products.append(dot(block, probes_ref[rows, :], (0, 0)))
        work_ref[leaf * KL : (leaf + 1) * KL, :] = shifted_gram(samples_products[leaf][:, :KL] / LEAF)
    inverse_factors(work_ref, panel_ref, COUNT)
    reduced_samples, reduced_probes = [], []
    for leaf in range(COUNT):
        rows = slice(leaf * LEAF, (leaf + 1) * LEAF)
        inverse = work_ref[leaf * KL : (leaf + 1) * KL, :]
        basis_ref[rows, :] = dot(remaining_ref[rows, :KL], inverse, (1, 1)).astype(bf16)
        reduced_samples.append(dot(inverse, samples_products[leaf], (1, 0)) / LEAF)
        reduced_probes.append(dot(inverse, probes_products[leaf], (1, 0)) / math.sqrt(LEAF))
    for leaf in range(COUNT):
        gram = dot(reduced_probes[leaf], reduced_probes[leaf], (1, 1)) / COLS
        work_ref[leaf * KL : (leaf + 1) * KL, :] = shifted_gram(gram)
    inverse_factors(work_ref, panel_ref, COUNT)
    for leaf in range(COUNT):
        sibling = leaf ^ 1
        rows = slice(leaf * KL, (leaf + 1) * KL)
        inverse = work_ref[sibling * KL : (sibling + 1) * KL, :]
        cross = dot(reduced_samples[leaf], reduced_probes[sibling], (1, 1)) / COLS
        coupling = dot(dot(cross, inverse, (1, 1)), inverse, (1, 0))
        coupling_ref[rows, :] = coupling.astype(bf16)
        parent_ref[rows, :] = reduced_samples[leaf][:, :KL] - dot(coupling, reduced_probes[sibling][:, :KL], (1, 0))
    gram_ref[...] = dot(parent_ref[...], parent_ref[...], (0, 0))


def parent_kernel(gram_ref, parent_ref, out_ref, work_ref, panel_ref):
    work_ref[...] = shifted_gram(gram_ref[...] / (LEAVES * KL))
    inverse_factors(work_ref, panel_ref, 1)
    out_ref[...] = dot(parent_ref[...], work_ref[...], (1, 1))


def whole(memory_space=pltpu.VMEM):
    return pl.BlockSpec(memory_space=memory_space)


def exchange(block, axes):
    size = lax.axis_size(axes)
    return lax.all_to_all(jnp.broadcast_to(block, (size,) + block.shape), axes, 0, 0)


def total(block):
    size = lax.axis_size("z")
    parts = lax.all_to_all(block.reshape(size, KL // size, KL), "z", 0, 0).sum(0)
    parts = exchange(parts, ("x", "c")).sum(0)
    parts = exchange(parts, "y").sum(0)
    return exchange(parts, "z").reshape(KL, KL)


def shifted(block, distance):
    devices = range(lax.axis_size(AXES))
    route = [(i - distance, i) for i in devices if i - distance in devices]
    return lax.ppermute(block, AXES, route)


def body(points, probes, samples, near_mask):
    size = COUNT * LEAF
    before = shifted(probes[2 * LEAF :], 1)
    after = shifted(probes[: 2 * LEAF], -1)
    before_points = shifted(points[:, 2 * LEAF :], 1)
    after_points = shifted(points[:, : 2 * LEAF], -1)
    smem, vmem = whole(pltpu.SMEM), whole()
    params = pltpu.CompilerParams(vmem_limit_bytes=VMEM_LIMIT)
    partial = pl.pallas_call(
        local_kernel,
        out_shape=jax.ShapeDtypeStruct((size, COLS), f32),
        in_specs=[smem, vmem, vmem, vmem],
        out_specs=vmem,
        scratch_shapes=[
            pltpu.VMEM((size, FEATURES), bf16),
            pltpu.VMEM((FEATURES, size), bf16),
            pltpu.VMEM((size, COLS), bf16),
            pltpu.VMEM((size, COLS), bf16),
        ],
        compiler_params=params,
        cost_estimate=pl.CostEstimate(flops=14 * 8 * LEAF * LEAF * COLS, bytes_accessed=6 << 20, transcendentals=28 * LEAF * LEAF),
        name="local_blocks",
    )(near_mask, points, probes, samples)
    basis, coupling, parent_rows, gram = pl.pallas_call(
        halo_kernel,
        out_shape=[
            jax.ShapeDtypeStruct((size, KL), bf16),
            jax.ShapeDtypeStruct((COUNT * KL, KL), bf16),
            jax.ShapeDtypeStruct((COUNT * KL, KL), f32),
            jax.ShapeDtypeStruct((KL, KL), f32),
        ],
        in_specs=[smem] + [vmem] * 7,
        out_specs=[vmem] * 4,
        scratch_shapes=[
            pltpu.VMEM((size, FEATURES), bf16),
            pltpu.VMEM((FEATURES, size), bf16),
            pltpu.VMEM((size, COLS), bf16),
            pltpu.VMEM((size, COLS), bf16),
            pltpu.VMEM((size, COLS), f32),
            pltpu.VMEM((COUNT * KL, KL), f32),
            pltpu.VMEM((COUNT * PANEL, KL), f32),
        ],
        compiler_params=params,
        name="halo_blocks",
    )(near_mask, points, before_points, after_points, partial, probes, before, after)
    parent_basis = pl.pallas_call(
        parent_kernel,
        out_shape=jax.ShapeDtypeStruct((COUNT * KL, KL), f32),
        in_specs=[vmem, vmem],
        out_specs=vmem,
        scratch_shapes=[pltpu.VMEM((KL, KL), f32), pltpu.VMEM((PANEL, KL), f32)],
        compiler_params=params,
        name="parent",
    )(total(gram), parent_rows)
    return basis, coupling, parent_basis


def solution(mesh):
    fine = Mesh(mesh.devices.reshape(8, 4, 8, 2), AXES)
    return jax.shard_map(
        body,
        mesh=fine,
        in_specs=(P(None, AXES), P(AXES, None), P(AXES, None), P(AXES, None)),
        out_specs=(P(AXES, None), P(AXES, None), P(AXES, None)),
        check_vma=False,
    )
```

```python
import functools
import math

import jax
import jax.numpy as jnp
from jax import lax
from jax.experimental import pallas as pl
from jax.experimental.pallas import tpu as pltpu
from jax.sharding import Mesh, PartitionSpec as P

LEAF = 512
COLS = 256
KL = 128
COUNT = 4
LEAVES = 2048
FEATURES = 32
PANEL = 16
HALF = 256
EXTRA = 16

AMPLITUDE = 0.25
SHIFT_RATIO = 0.01
EPSILON = 1e-05
LOG2E = math.log2(math.e)
SCALE = math.sqrt(3.0) * LOG2E
WEIGHT = AMPLITUDE / LOG2E

highest = lax.Precision.HIGHEST
f32 = jnp.float32
bf16 = jnp.bfloat16
AXES = ("z", "x", "y", "c")
VMEM_LIMIT = 48 * 1024 * 1024


def split2(values):
    high = values.astype(bf16)
    low = (values - high.astype(f32)).astype(bf16)
    return high, low


def split3(values):
    high = values.astype(bf16)
    rest = values - high.astype(f32)
    middle = rest.astype(bf16)
    low = (rest - middle.astype(f32)).astype(bf16)
    return high, middle, low


def dot(left, right, contract, precision=highest):
    return lax.dot_general(
        left, right, ((contract[:1], contract[1:]), ((), ())),
        precision=precision, preferred_element_type=f32,
    )


def fast(left, right, contract):
    return dot(left, right, contract, None)


def features(points, target):
    rows = [points[d : d + 1, :] for d in range(3)]
    norm = [piece.astype(f32) for piece in split3(rows[0] * rows[0] + rows[1] * rows[1] + rows[2] * rows[2])]
    ones = jnp.ones_like(rows[0])
    out = []
    for row in rows:
        pieces = [piece.astype(f32) for piece in split3(row)]
        if target:
            out += [pieces[i] for i in (0, 0, 1, 1, 0, 2)]
        else:
            out += [-2.0 * pieces[i] for i in (0, 1, 0, 1, 2, 0)]
    out += norm + [ones] * 3 if target else [ones] * 3 + norm
    out += [jnp.zeros_like(ones)] * (FEATURES - len(out))
    return jnp.concatenate(out, axis=0)


def dot3(left, right, contract):
    left_high, left_low = split2(left)
    right_high, right_low = split2(right)
    return fast(
        jnp.concatenate([left_high, left_low, left_high], axis=contract[0]),
        jnp.concatenate([right_high, right_high, right_low], axis=contract[1]),
        contract,
    )


def near_blocks(targets_ref, sources_ref, high_ref, low_ref, ahead_ref, out_ref, mask_ref, number, pair_of):
    def distances(target, source, half):
        rows = pl.ds(pl.multiple_of(target * LEAF, LEAF), LEAF)
        columns = pl.ds(pl.multiple_of(source * LEAF + half * HALF, HALF), HALF)
        return fast(targets_ref[rows, :], sources_ref[:, columns], (1, 0))

    def product(squared, source, half):
        rows = pl.ds(pl.multiple_of(source * LEAF + half * HALF, HALF), HALF)
        high_probes, low_probes = high_ref[rows, :], low_ref[rows, :]
        squared = jnp.maximum(squared, 1e-24)
        scaled = squared * lax.rsqrt(squared)
        high, low = split2((scaled + LOG2E) * jnp.exp2(-scaled))
        return fast(
            jnp.concatenate([high, low, high], axis=1),
            jnp.concatenate([high_probes, high_probes, low_probes], axis=0),
            (1, 0),
        )

    def loop(pair, _):
        target, source, offset = pair_of(pair)
        next_target, next_source, _ = pair_of(jnp.minimum(pair + 1, number - 1))
        slot = jnp.clip(jnp.where(offset < 0, offset + 2, offset + 1), 0, 3)
        weight = jnp.where(offset == 0, 1, mask_ref[target, slot]).astype(f32) * WEIGHT
        second = distances(target, source, 1)
        term = product(ahead_ref[...], source, 0)
        ahead_ref[...] = distances(next_target, next_source, 0)
        term += product(second, source, 1)
        rows = pl.ds(pl.multiple_of(target * LEAF, LEAF), LEAF)
        out_ref[rows, :] -= weight * term
        return 0

    first_target, first_source, _ = pair_of(0)
    ahead_ref[...] = distances(first_target, first_source, 0)
    lax.fori_loop(0, number, loop, 0)


def after(pair, *limits):
    return sum(jnp.where(pair >= limit, 1, 0) for limit in limits)


def local_pair(pair):
    target = after(pair, 3, 7, 11)
    source = pair - 3 * after(pair, 3) - 4 * after(pair, 7) - 3 * after(pair, 11)
    return target, source, source - target


def halo_pair(pair):
    target = pair - after(pair, 1, 5)
    source = (pair + 1) // 2
    return target, source, jnp.where(source < 2, source - 2, source + 2) - target


def local_kernel(mask_ref, points_ref, probes_ref, samples_ref, out_ref, targets_ref, sources_ref, high_ref, low_ref, ahead_ref):
    centred = (points_ref[...] - points_ref[:, 0:1]) * SCALE
    targets_ref[...] = features(centred, True).T.astype(bf16)
    sources_ref[...] = features(centred, False).astype(bf16)
    high, low = split2(probes_ref[...])
    high_ref[...] = high
    low_ref[...] = low
    out_ref[...] = samples_ref[...]
    near_blocks(targets_ref, sources_ref, high_ref, low_ref, ahead_ref, out_ref, mask_ref, 14, local_pair)


def shifted_gram(gram):
    row = lax.broadcasted_iota(jnp.int32, (KL, KL), 0)
    column = lax.broadcasted_iota(jnp.int32, (KL, KL), 1)
    diagonal = row == column
    trace = jnp.sum(jnp.where(diagonal, gram, 0.0))
    return gram + jnp.where(diagonal, SHIFT_RATIO * trace / KL + EPSILON, 0.0)


def inverse_factors(work_ref, panel_ref, number, beside=()):
    lane = lax.broadcasted_iota(jnp.int32, (number, KL), 1)
    wide_lane = lax.broadcasted_iota(jnp.int32, (KL, KL), 1)
    for first in range(0, KL, PANEL):
        rows = [work_ref[pl.ds(first + j, number, stride=KL), :] for j in range(PANEL)]
        entry = {
            (j, i): jnp.broadcast_to(rows[j][:, first + i : first + i + 1], (number, KL))
            for j in range(PANEL)
            for i in range(j, PANEL)
        }
        if first // PANEL < len(beside):
            beside[first // PANEL]()
        inside = (lane >= first) & (lane < first + PANEL)
        rows = [jnp.where(inside, jnp.where(lane == first + j, 1.0, 0.0), rows[j]) for j in range(PANEL)]
        for k in range(PANEL):
            scale = lax.rsqrt(entry[k, k])
            rows[k] = rows[k] * scale
            factor = {j: entry[k, j] * scale for j in range(k + 1, PANEL)}
            for j in range(k + 1, PANEL):
                for i in range(j, PANEL):
                    entry[j, i] = entry[j, i] - factor[j] * factor[i]
                rows[j] = rows[j] - factor[j] * rows[k]
            panel_ref[pl.ds(k, number, stride=PANEL), :] = rows[k]
        stop = first + PANEL
        for matrix in range(number):
            panel = panel_ref[matrix * PANEL : (matrix + 1) * PANEL, :]
            base = matrix * KL
            work_ref[base + first : base + stop, :] = jnp.where(
                wide_lane[:PANEL] < stop, panel, 0.0
            )
            if stop < KL:
                high, middle, low = split3(panel)
                left = jnp.concatenate([high, high, middle, middle, high, low], axis=0)
                right = jnp.concatenate([high, middle, high, middle, low, high], axis=0)
                update = fast(left, right, (0, 0))
                done = (wide_lane >= first) & (wide_lane < stop)
                old = jnp.where(done[stop:], 0.0, work_ref[base + stop : base + KL, :])
                work_ref[base + stop : base + KL, :] = old - update[stop:, :]


def halo_kernel(
    mask_ref, points_ref, partial_ref, probes_ref, before_ref, after_ref,
    basis_ref, coupling_ref, parent_ref, gram_ref,
    targets_ref, sources_ref, high_ref, low_ref, ahead_ref, remaining_ref, work_ref, panel_ref,
):
    size = 2 * LEAF
    centre = points_ref[:, 0:1]
    targets_ref[...] = features((points_ref[...] - centre) * SCALE, True).T.astype(bf16)
    for half, halo_ref in enumerate((before_ref, after_ref)):
        columns = slice(half * size, (half + 1) * size)
        parts = size // COLS
        halo_points = jnp.concatenate(
            [
                jnp.concatenate([halo_ref[size + d * parts + p : size + d * parts + p + 1, :] for p in range(parts)], axis=1)
                for d in range(3)
            ],
            axis=0,
        )
        sources_ref[:, columns] = features((halo_points - centre) * SCALE, False).astype(bf16)
        high, low = split2(halo_ref[:size, :])
        high_ref[columns, :] = high
        low_ref[columns, :] = low
    remaining_ref[...] = partial_ref[...]
    near_blocks(targets_ref, sources_ref, high_ref, low_ref, ahead_ref, remaining_ref, mask_ref, 6, halo_pair)

    leaves = range(COUNT)
    points_of = [slice(leaf * LEAF, (leaf + 1) * LEAF) for leaf in leaves]
    ranks_of = [slice(leaf * KL, (leaf + 1) * KL) for leaf in leaves]
    samples_products, probes_products = [], [None] * COUNT
    for leaf in leaves:
        rows = points_of[leaf]
        samples_products.append(dot(remaining_ref[rows, :KL], remaining_ref[rows, :], (0, 0)))
        work_ref[ranks_of[leaf], :] = shifted_gram(samples_products[leaf][:, :KL] / LEAF)

    def make_probes_product(leaf):
        rows = points_of[leaf]
        probes_products[leaf] = dot(remaining_ref[rows, :KL], probes_ref[rows, :], (0, 0))

    inverse_factors(work_ref, panel_ref, COUNT, [functools.partial(make_probes_product, leaf) for leaf in leaves])
    inverses = [work_ref[rows, :] for rows in ranks_of]
    reduced_probes, reduced_samples, crosses = [], [None] * COUNT, [None] * COUNT
    for leaf in leaves:
        reduced_probes.append(dot(inverses[leaf], probes_products[leaf], (1, 0)) / math.sqrt(LEAF))
        gram = dot(reduced_probes[leaf], reduced_probes[leaf], (1, 1)) / COLS
        work_ref[ranks_of[leaf], :] = shifted_gram(gram)

    def make_cross(leaf):
        reduced_samples[leaf] = dot(inverses[leaf], samples_products[leaf], (1, 0)) / LEAF
        crosses[leaf] = dot(reduced_samples[leaf], reduced_probes[leaf ^ 1], (1, 1)) / COLS

    def make_basis(leaf):
        rows = points_of[leaf]
        basis_ref[rows, :] = dot3(remaining_ref[rows, :KL], inverses[leaf], (1, 1)).astype(bf16)

    beside = [functools.partial(make, leaf) for make in (make_cross, make_basis) for leaf in leaves]
    inverse_factors(work_ref, panel_ref, COUNT, beside)
    for leaf in leaves:
        sibling = leaf ^ 1
        inverse = work_ref[ranks_of[sibling], :]
        coupling = dot(dot(crosses[leaf], inverse, (1, 1)), inverse, (1, 0))
        coupling_ref[ranks_of[leaf], :] = coupling.astype(bf16)
        parent_ref[ranks_of[leaf], :] = reduced_samples[leaf][:, :KL] - dot(
            coupling, reduced_probes[sibling][:, :KL], (1, 0)
        )
    gram_ref[...] = dot(parent_ref[...], parent_ref[...], (0, 0))


def parent_kernel(gram_ref, parent_ref, out_ref, work_ref, panel_ref):
    work_ref[...] = shifted_gram(gram_ref[...] / (LEAVES * KL))
    inverse_factors(work_ref, panel_ref, 1)
    out_ref[...] = dot3(parent_ref[...], work_ref[...], (1, 1))


def whole(memory_space=pltpu.VMEM):
    return pl.BlockSpec(memory_space=memory_space)


def exchange(block, axes):
    size = lax.axis_size(axes)
    return lax.all_to_all(jnp.broadcast_to(block, (size,) + block.shape), axes, 0, 0)


def total(block):
    near = ("x", "c")
    size = lax.axis_size(near)
    parts = lax.all_to_all(block.reshape(size, KL // size, KL), near, 0, 0).sum(0)
    parts = exchange(parts, "y").sum(0)
    parts = exchange(parts, "z").sum(0)
    return exchange(parts, near).reshape(KL, KL)


def shifted(block, distance):
    devices = range(lax.axis_size(AXES))
    route = [(i - distance, i) for i in devices if i - distance in devices]
    return lax.ppermute(block, AXES, route)


def packed(points, probes):
    rows = points.reshape(-1, COLS)
    return jnp.concatenate([probes, jnp.pad(rows, ((0, EXTRA - rows.shape[0]), (0, 0)))], axis=0)


def body(points, probes, samples, near_mask):
    size = COUNT * LEAF
    smem, vmem = whole(pltpu.SMEM), whole()
    params = pltpu.CompilerParams(vmem_limit_bytes=VMEM_LIMIT)
    up, down = (packed(points[:, part], probes[part]) for part in (slice(2 * LEAF, size), slice(0, 2 * LEAF)))
    before, after_block = shifted(up, 1), shifted(down, -1)
    near_scratch = [
        pltpu.VMEM((size, FEATURES), bf16),
        pltpu.VMEM((FEATURES, size), bf16),
        pltpu.VMEM((size, COLS), bf16),
        pltpu.VMEM((size, COLS), bf16),
        pltpu.VMEM((LEAF, HALF), f32),
    ]
    partial = pl.pallas_call(
        local_kernel,
        out_shape=jax.ShapeDtypeStruct((size, COLS), f32),
        in_specs=[smem, vmem, vmem, vmem],
        out_specs=vmem,
        scratch_shapes=near_scratch,
        compiler_params=params,
        cost_estimate=pl.CostEstimate(flops=14 * 8 * LEAF * LEAF * COLS, bytes_accessed=6 << 20, transcendentals=28 * LEAF * LEAF),
        name="local_blocks",
    )(near_mask, points, probes, samples)
    basis, coupling, parent_rows, gram = pl.pallas_call(
        halo_kernel,
        out_shape=[
            jax.ShapeDtypeStruct((size, KL), bf16),
            jax.ShapeDtypeStruct((COUNT * KL, KL), bf16),
            jax.ShapeDtypeStruct((COUNT * KL, KL), f32),
            jax.ShapeDtypeStruct((KL, KL), f32),
        ],
        in_specs=[smem] + [vmem] * 5,
        out_specs=[vmem] * 4,
        scratch_shapes=near_scratch + [
            pltpu.VMEM((size, COLS), f32),
            pltpu.VMEM((COUNT * KL, KL), f32),
            pltpu.VMEM((COUNT * PANEL, KL), f32),
        ],
        compiler_params=params,
        name="halo_blocks",
    )(near_mask, points, partial, probes, before, after_block)
    parent_basis = pl.pallas_call(
        parent_kernel,
        out_shape=jax.ShapeDtypeStruct((COUNT * KL, KL), f32),
        in_specs=[vmem, vmem],
        out_specs=vmem,
        scratch_shapes=[pltpu.VMEM((KL, KL), f32), pltpu.VMEM((PANEL, KL), f32)],
        compiler_params=params,
        name="parent",
    )(total(gram), parent_rows)
    return basis, coupling, parent_basis


def solution(mesh):
    fine = Mesh(mesh.devices.reshape(8, 4, 8, 2), AXES)
    return jax.shard_map(
        body,
        mesh=fine,
        in_specs=(P(None, AXES), P(AXES, None), P(AXES, None), P(AXES, None)),
        out_specs=(P(AXES, None), P(AXES, None), P(AXES, None)),
        check_vma=False,
    )
```
